256 devices in a mesh: dp: 8 (over z), expert: 16 (over y, x), pipe: 2 (over core).
Axes of the slice: x: 4, y: 4, z: 8, core: 2. Of those that a mesh axis runs over, the one named last changes fastest.
Arguments:
- layer_io: bfloat16 [2, 2, 4096, 7168], P('pipe', None, ('dp', 'expert')), may hold values from -6 to 6
- route_ids: int32 [2, 2, 4096, 8], P('pipe', None, ('dp', 'expert')), may hold values from 0 to 63, all different within a row
- route_weights: float32 [2, 2, 4096, 8], P('pipe', None, ('dp', 'expert')), may hold values from 0.1 to 0.5
- gate_weight: bfloat16 [2, 16, 7168, 1024], P('pipe', 'expert', 'dp'), may hold values from -0.0625 to 0.0625
- up_weight: bfloat16 [2, 16, 7168, 1024], P('pipe', 'expert', 'dp'), may hold values from -0.0625 to 0.0625
- down_weight: bfloat16 [2, 16, 1024, 7168], P('pipe', 'expert', None, 'dp'), may hold values from -0.1875 to 0.1875
Outputs:
- layer_out: bfloat16 [2, 2, 4096, 7168], P('pipe', None, ('dp', 'expert'))
- grad_gate_weight: bfloat16 [2, 16, 7168, 1024], P('pipe', 'expert', 'dp')
- grad_up_weight: bfloat16 [2, 16, 7168, 1024], P('pipe', 'expert', 'dp')
- grad_down_weight: bfloat16 [2, 16, 1024, 7168], P('pipe', 'expert', None, 'dp')
The draws below stay inside these ranges and needn't reach their ends.
All inputs are finite; a program needn't handle non-finite values.
Results may differ from the reference program's by a relative error of at most 0.039.
Values may be sent and summed in bfloat16 or wider, within the bound.
No kernel may reach another device: no remote copies, remote signals or barrier semaphores. Data moves between devices by JAX's collectives and lax.ppermute only.
A program may use at most 128 MiB of HBM per device.

```python
import jax
import jax.numpy as jnp
from jax import lax

D = 7168
FF = 1024
ROUTED = 64
TOP = 8
MICRO = 2
CAPACITY = 2
TOK_DEV = 32
EXPERTS = 16
LAYERS = 2
TOKENS = 4096


def shard_levels(rng, extent, shards, smallest, largest):
    loudness = 1.0
    for axis_at, blocks in shards:
        draws = jax.random.uniform(jax.random.fold_in(jax.random.fold_in(rng, 6), axis_at), (blocks,), jnp.float32, smallest / len(shards), largest / len(shards))
        loudness = loudness * jnp.repeat(jnp.exp(draws), extent[axis_at] // blocks).reshape((-1,) + (1,) * (len(extent) - 1 - axis_at))
    return loudness


def picks_of(key, rows, amount, top, lift):
    order = jax.random.permutation(jax.random.fold_in(key, 1), amount)
    boost = order
    for power in range(3):
        boost = boost * boost // amount
    boost = boost * lift // amount
    lots = jax.random.randint(jax.random.fold_in(key, 2), (rows, amount), 0, 4096) + boost
    fixed_rows = jax.random.permutation(jax.random.fold_in(key, 3), rows)[jnp.arange(amount) % rows]
    lots = jnp.where(jnp.arange(rows)[:, None] == fixed_rows[None, :], 1 << 14, lots)
    merit = lots * amount + jnp.arange(amount)
    return lax.top_k(merit.astype(jnp.int32), top)[1].astype(jnp.int32)


def bell_draw(key, shape, deviation, limit, cuts=(), held_as=jnp.bfloat16):
    drawn = jax.random.normal(key, shape, jnp.float32) * deviation
    if len(cuts) > 0:
        drawn = shard_levels(key, shape, cuts, -0.22, 0.18) * drawn
    return jnp.clip(drawn, min=-limit, max=limit).astype(held_as)


def setup_inputs(seed: int = 0) -> dict:
    keys = jax.random.split(jax.random.key(seed), 7)
    return {
        "layer_io": bell_draw(keys[0], (2, MICRO, TOKENS, D), 1.0, 6.0, ((0, 2), (2, 128))),
        "route_ids": picks_of(keys[1], LAYERS * MICRO * TOKENS, ROUTED, TOP, 2048).reshape((LAYERS, MICRO, TOKENS, TOP)),
        "route_weights": jnp.clip(0.1 + 0.4 * jax.random.uniform(keys[2], (LAYERS, MICRO, TOKENS, TOP), jnp.float32) ** shard_levels(keys[2], (LAYERS, MICRO, TOKENS, TOP), ((0, 2), (2, 128)), -0.2, 0.2), 0.1, 0.5),
        "gate_weight": bell_draw(keys[3], (LAYERS, EXPERTS, D, FF), D ** -0.5, 0.0625, ((0, 2), (1, 16), (2, 8))),
        "up_weight": bell_draw(keys[4], (LAYERS, EXPERTS, D, FF), D ** -0.5, 0.0625, ((0, 2), (1, 16), (2, 8))),
        "down_weight": bell_draw(keys[5], (LAYERS, EXPERTS, FF, D), FF ** -0.5, 0.1875, ((0, 2), (1, 16), (3, 8))),
    }


def route_tables(chosen_ids):
    blocks = TOKENS // TOK_DEV
    flat_ids = chosen_ids.reshape(blocks, TOK_DEV * TOP).astype(jnp.int32)
    onehot = (flat_ids[:, :, None] == jnp.arange(ROUTED, dtype=jnp.int32)[None, None, :]).astype(jnp.int32)
    before = (jnp.cumsum(onehot, axis=1) - onehot).astype(jnp.int32)
    position = jnp.sum(before * onehot, axis=2).astype(jnp.int32)
    keep_mask = (flat_ids < EXPERTS) & (position < CAPACITY)
    expert_index = jnp.where(keep_mask, flat_ids, EXPERTS).reshape(-1).astype(jnp.int32)
    block_index = jnp.broadcast_to(jnp.arange(blocks, dtype=jnp.int32)[:, None], flat_ids.shape).reshape(-1)
    slot_index = jnp.where(keep_mask, position, 0).reshape(-1).astype(jnp.int32)
    return expert_index, block_index, slot_index, keep_mask.reshape(TOKENS, TOP)


def scatter_rows(spread, tables):
    expert_index, block_index, slot_index, keep_mask = tables
    blocks = TOKENS // TOK_DEV
    empty = jnp.zeros((EXPERTS, blocks, CAPACITY, spread.shape[1]), spread.dtype)
    filled = empty.at[expert_index, block_index, slot_index].add(spread, mode="drop")
    return filled.reshape(EXPERTS, blocks * CAPACITY, spread.shape[1])


def gather_rows(buffers, tables, scale):
    expert_index, block_index, slot_index, keep_mask = tables
    blocks = TOKENS // TOK_DEV
    shaped = buffers.reshape(EXPERTS, blocks, CAPACITY, buffers.shape[2])
    picked = shaped[jnp.minimum(expert_index, EXPERTS - 1), block_index, slot_index].astype(jnp.float32)
    factor = jnp.where(keep_mask, scale, jnp.zeros_like(scale)).reshape(-1, 1)
    return jnp.sum((picked * factor).reshape(TOKENS, TOP, -1), axis=1)


def expert_forward(operands):
    rows, gate_part, up_part, down_part = operands
    gate = jnp.dot(rows, gate_part, preferred_element_type=jnp.float32)
    up = jnp.dot(rows, up_part, preferred_element_type=jnp.float32)
    hidden = (jax.nn.silu(gate) * up).astype(jnp.bfloat16)
    output = jnp.dot(hidden, down_part, preferred_element_type=jnp.float32).astype(jnp.bfloat16)
    return output, gate, up, hidden


def expert_backward(operands):
    rows, gate, up, hidden, grad_out, gate_part, up_part, down_part = operands

    def one_micro(carry, item):
        rows_one, gate_one, up_one, hidden_one, grad_one = item
        grad_hidden = jnp.dot(grad_one, down_part.T, preferred_element_type=jnp.float32)
        sigmoid_gate = jax.nn.sigmoid(gate_one)
        grad_gate = (grad_hidden * up_one * sigmoid_gate * (1.0 + gate_one * (1.0 - sigmoid_gate))).astype(jnp.bfloat16)
        grad_up = (grad_hidden * gate_one * sigmoid_gate).astype(jnp.bfloat16)
        sum_gate = carry[0] + jnp.dot(rows_one.T, grad_gate, preferred_element_type=jnp.float32)
        sum_up = carry[1] + jnp.dot(rows_one.T, grad_up, preferred_element_type=jnp.float32)
        sum_down = carry[2] + jnp.dot(hidden_one.T, grad_one, preferred_element_type=jnp.float32)
        grad_rows = (jnp.dot(grad_gate, gate_part.T, preferred_element_type=jnp.float32)
                     + jnp.dot(grad_up, up_part.T, preferred_element_type=jnp.float32)).astype(jnp.bfloat16)
        return (sum_gate, sum_up, sum_down), grad_rows

    start = (jnp.zeros(gate_part.shape, jnp.float32), jnp.zeros(up_part.shape, jnp.float32),
             jnp.zeros(down_part.shape, jnp.float32))
    sums, grad_rows = lax.scan(one_micro, start, (rows, gate, up, hidden, grad_out))
    return grad_rows, sums[0].astype(jnp.bfloat16), sums[1].astype(jnp.bfloat16), sums[2].astype(jnp.bfloat16)


def reference(layer_io, route_ids, route_weights, gate_weight, up_weight, down_weight):
    current = [layer_io[0, micro_index] for micro_index in range(MICRO)]
    saved = []
    for layer in range(LAYERS):
        layer_saved = []
        following = []
        for micro_index in range(MICRO):
            tables = route_tables(route_ids[layer, micro_index])
            rows = scatter_rows(jnp.repeat(current[micro_index], TOP, axis=0), tables)
            output, gate, up, hidden = lax.map(expert_forward, (rows, gate_weight[layer], up_weight[layer], down_weight[layer]))
            mixed = gather_rows(output, tables, route_weights[layer, micro_index])
            following.append((current[micro_index].astype(jnp.float32) + mixed).astype(jnp.bfloat16))
            layer_saved.append((tables, rows, gate, up, hidden))
        saved.append(layer_saved)
        current = following
    finals = current
    upstream = [layer_io[1, micro_index] for micro_index in range(MICRO)]
    grads_gate = [None] * LAYERS
    grads_up = [None] * LAYERS
    grads_down = [None] * LAYERS
    for layer in reversed(range(LAYERS)):
        grad_in = []
        for micro_index in range(MICRO):
            tables = saved[layer][micro_index][0]
            scaled = route_weights[layer, micro_index].reshape(-1, 1) * jnp.repeat(upstream[micro_index].astype(jnp.float32), TOP, axis=0)
            grad_in.append(scatter_rows(scaled.astype(jnp.bfloat16), tables))
        stacked_rows = jnp.stack([saved[layer][micro_index][1] for micro_index in range(MICRO)], axis=1)
        stacked_gate = jnp.stack([saved[layer][micro_index][2] for micro_index in range(MICRO)], axis=1)
        stacked_up = jnp.stack([saved[layer][micro_index][3] for micro_index in range(MICRO)], axis=1)
        stacked_hidden = jnp.stack([saved[layer][micro_index][4] for micro_index in range(MICRO)], axis=1)
        grad_rows, grads_gate[layer], grads_up[layer], grads_down[layer] = lax.map(
            expert_backward, (stacked_rows, stacked_gate, stacked_up, stacked_hidden, jnp.stack(grad_in, axis=1),
                              gate_weight[layer], up_weight[layer], down_weight[layer]))
        updated = []
        for micro_index in range(MICRO):
            tables = saved[layer][micro_index][0]
            ones = jnp.ones_like(route_weights[layer, micro_index])
            back = gather_rows(grad_rows[:, micro_index], tables, ones)
            updated.append((upstream[micro_index].astype(jnp.float32) + back).astype(jnp.bfloat16))
        upstream = updated
    layer_out = jnp.stack([jnp.stack(upstream), jnp.stack(finals)])
    return layer_out, jnp.stack(grads_gate), jnp.stack(grads_up), jnp.stack(grads_down)
```

```python
import jax
import jax.numpy as jnp
from jax import lax
from jax.sharding import PartitionSpec as P

CAPACITY = 2
LAYERS = 2
ROUTE_COLUMNS = 128

highest = lax.Precision.HIGHEST
bf16 = jnp.bfloat16
f32 = jnp.float32


def swap(values, axes):
    return lax.all_to_all(values, axes, split_axis=0, concat_axis=0, tiled=True)


def trade_cores(values):
    return lax.ppermute(values, "pipe", [(0, 1), (1, 0)])


def dot(a, b, contract):
    return lax.dot_general(a, b, ((contract[:1], contract[1:]), ((), ())), preferred_element_type=f32)


def route_columns(ids, weights, experts):
    tokens = ids.shape[1]
    hit = ids[..., None] == jnp.arange(experts, dtype=jnp.int32)
    chosen = jnp.any(hit, axis=2).astype(f32)
    weight = jnp.sum(jnp.where(hit, weights[..., None], 0.0), axis=2)
    earlier = (jnp.arange(tokens)[:, None] > jnp.arange(tokens)[None, :]).astype(f32)
    before = jnp.einsum("ts,mse->mte", earlier, chosen)
    code = jnp.where((chosen > 0) & (before < CAPACITY), before + 1.0, 0.0)
    high = lax.reduce_precision(weight, 8, 7)
    rest = weight - high
    middle = lax.reduce_precision(rest, 8, 7)
    low = rest - middle
    columns = jnp.concatenate([code, high, middle, low], axis=-1).astype(bf16)
    return jnp.pad(columns, ((0, 0), (0, 0), (0, ROUTE_COLUMNS - columns.shape[-1])))


def routing(columns, groups, experts):
    tokens = columns.shape[0]
    rows = experts * groups * CAPACITY
    row = jnp.arange(rows, dtype=jnp.int32)
    per_expert = groups * CAPACITY
    spread = (row[:, None] // per_expert == jnp.arange(experts)[None, :]).astype(bf16)
    parts = [columns[:, i * experts : (i + 1) * experts] for i in range(4)]
    code, high, middle, low = [dot(spread, part, (1, 1)) for part in parts]
    same_block = (row[:, None] % per_expert) // CAPACITY == (
        jnp.arange(tokens, dtype=jnp.int32)[None, :] // (tokens // groups)
    )
    slot = (row % CAPACITY + 1).astype(f32)
    mask = same_block & (code == slot[:, None])
    return mask.astype(bf16), jnp.where(mask, high + middle + low, 0.0)


def sum_over_dp(partial, groups):
    rows, width = partial.shape
    moved = swap(partial.reshape(groups, rows // groups, width), "dp")
    return jnp.sum(moved.astype(f32), axis=0)


def gather_over_dp(own, groups):
    moved = swap(jnp.broadcast_to(own[None], (groups,) + own.shape), "dp")
    return moved.reshape(groups * own.shape[0], own.shape[1])


def to_experts(rows, experts):
    moved = swap(rows.reshape(experts, rows.shape[0] // experts, rows.shape[1]), "expert")
    return moved.reshape(rows.shape)


def gradients_of(grad_hidden, gate, up):
    sig = jax.nn.sigmoid(gate)
    grad_gate = (grad_hidden * up * sig * (1.0 + gate * (1.0 - sig))).astype(bf16)
    grad_up = (grad_hidden * gate * sig).astype(bf16)
    return jnp.concatenate([grad_gate, grad_up], axis=1)


def shards(layer_io, route_ids, route_weights, gate_weight, up_weight, down_weight):
    groups = lax.axis_size("dp")
    experts = lax.axis_size("expert")
    first = lax.axis_index("pipe") == 0
    micro, tokens, width = layer_io.shape[1:]
    part = width // groups
    hidden_width = gate_weight.shape[3]

    other = [trade_cores(w) for w in (gate_weight[0, 0], up_weight[0, 0], down_weight[0, 0])]
    mine = [gate_weight[0, 0], up_weight[0, 0], down_weight[0, 0]]
    layer_weights = [
        [jnp.where(first, a, b) for a, b in zip(mine, other)],
        [jnp.where(first, b, a) for a, b in zip(mine, other)],
    ]
    gate_up = [jnp.concatenate(w[:2], axis=1) for w in layer_weights]
    down = [w[2] for w in layer_weights]

    columns = route_columns(route_ids[0], route_weights[0], experts)
    pieces = layer_io[0].reshape(micro, tokens, groups, part).transpose(2, 0, 1, 3)
    columns = jnp.broadcast_to(columns[None], (groups,) + columns.shape)
    sent = jnp.concatenate([pieces, columns], axis=3)
    got = swap(sent.reshape(groups * micro, tokens, part + ROUTE_COLUMNS), ("dp", "pipe"))
    got = got.reshape(groups, LAYERS, tokens, part + ROUTE_COLUMNS)
    inputs = got[:, 0, :, :part].reshape(groups * tokens, part)
    cotangent = got[:, 1, :, :part].reshape(groups * tokens, part)
    tables = [
        routing(got[:, l, :, part:].reshape(groups * tokens, ROUTE_COLUMNS), groups, experts)
        for l in range(LAYERS)
    ]

    def dispatch(placing, values):
        return to_experts(dot(placing, values, (1, 0)).astype(bf16), experts)

    def dispatch_scaled(placing, mixing, values):
        scale = jnp.sum(mixing, axis=1, keepdims=True)
        return to_experts((dot(placing, values, (1, 0)) * scale).astype(bf16), experts)

    def grad_hidden_of(grad_out, l):
        return sum_over_dp(dot(grad_out, down[l], (1, 1)).astype(bf16), groups)

    current = inputs
    rows, sums, hidden = [], [], []
    grad_out, grad_hidden = [None] * LAYERS, [None] * LAYERS
    for l in range(LAYERS):
        placing, mixing = tables[l]
        rows.append(dispatch(placing, current))
        sums.append(sum_over_dp(dot(rows[l], gate_up[l], (1, 0)).astype(bf16), groups))
        gate, up = sums[l][:, :hidden_width], sums[l][:, hidden_width:]
        hidden.append(gather_over_dp((jax.nn.silu(gate) * up).astype(bf16), groups))
        result = to_experts(dot(hidden[l], down[l], (1, 0)).astype(bf16), experts)
        mixed = lax.dot_general(
            mixing, result.astype(f32), (((0,), (0,)), ((), ())), precision=highest
        )
        current = (current.astype(f32) + mixed).astype(bf16)
    output = current

    upstream = cotangent
    grads = [None] * LAYERS
    for l in reversed(range(LAYERS)):
        placing, mixing = tables[l]
        grad_out[l] = dispatch_scaled(placing, mixing, upstream)
        grad_hidden[l] = grad_hidden_of(grad_out[l], l)
        gate, up = sums[l][:, :hidden_width], sums[l][:, hidden_width:]
        grads[l] = gather_over_dp(gradients_of(grad_hidden[l], gate, up), groups)
        back = to_experts(dot(grads[l], gate_up[l], (1, 1)).astype(bf16), experts)
        upstream = (upstream.astype(f32) + dot(placing, back, (0, 0))).astype(bf16)

    ends = jnp.stack([upstream.reshape(groups, tokens, part), output.reshape(groups, tokens, part)], axis=1)
    home = swap(ends.reshape(groups * LAYERS, tokens, part), ("dp", "pipe"))
    home = home.reshape(groups, micro, tokens, part).transpose(1, 2, 0, 3).reshape(micro, tokens, width)

    def own_and_other(pair):
        own = jnp.where(first, pair[0], pair[1])
        return own, trade_cores(jnp.where(first, pair[1], pair[0]))

    def weight_grad(left, right):
        return dot(left[0], right[0], (0, 0)) + dot(left[1], right[1], (0, 0))

    both_rows, both_grads = own_and_other(rows), own_and_other(grads)
    both_hidden, both_out = own_and_other(hidden), own_and_other(grad_out)
    grad_gate = weight_grad(both_rows, [g[:, :hidden_width] for g in both_grads])
    grad_up = weight_grad(both_rows, [g[:, hidden_width:] for g in both_grads])
    grad_down = weight_grad(both_hidden, both_out)
    return (
        home[None],
        grad_gate.astype(bf16)[None, None],
        grad_up.astype(bf16)[None, None],
        grad_down.astype(bf16)[None, None],
    )


def solution(mesh):
    tokens = P("pipe", None, ("dp", "expert"), None)
    inner = P("pipe", "expert", "dp", None)
    outer = P("pipe", "expert", None, "dp")
    return jax.shard_map(
        shards,
        mesh=mesh,
        in_specs=(tokens, tokens, tokens, inner, inner, outer),
        out_specs=(tokens, inner, inner, outer),
        check_vma=False,
    )
```

```python
import functools

import jax
import jax.numpy as jnp
from jax import lax
from jax.experimental import pallas as pl
from jax.experimental.pallas import tpu as pltpu
from jax.sharding import PartitionSpec as P

CAPACITY = 2
LAYERS = 2
ROUTE_COLUMNS = 128

highest = lax.Precision.HIGHEST
bf16 = jnp.bfloat16
f32 = jnp.float32
i32 = jnp.int32


def swap(values, axes):
    return lax.all_to_all(values, axes, split_axis=0, concat_axis=0, tiled=True)


def trade_cores(values):
    return lax.ppermute(values, "pipe", [(0, 1), (1, 0)])


def dot(a, b, contract):
    return lax.dot_general(a, b, ((contract[:1], contract[1:]), ((), ())), preferred_element_type=f32)


def local(body, dims, operands, name):
    return pl.pallas_call(
        body,
        out_shape=jax.ShapeDtypeStruct(dims, bf16),
        compiler_params=pltpu.CompilerParams(vmem_limit_bytes=32 * 1024 * 1024),
        name=name,
    )(*operands)


def exact_parts(values):
    high = values.astype(bf16)
    rest = values - high.astype(f32)
    middle = rest.astype(bf16)
    return high, middle, (rest - middle.astype(f32)).astype(bf16)


def pack_body(experts, groups, io, ids, weights, sent):
    micro, tokens, width = io.shape
    part = width // groups
    column = lax.broadcasted_iota(i32, (tokens, ROUTE_COLUMNS), 1)
    expert, kind = column % experts, column // experts
    later = lax.broadcasted_iota(i32, (tokens, tokens), 0)
    earlier = (lax.broadcasted_iota(i32, (tokens, tokens), 1) < later).astype(f32).astype(bf16)
    for m in range(micro):
        chosen = jnp.zeros((tokens, ROUTE_COLUMNS), f32)
        weight = jnp.zeros((tokens, ROUTE_COLUMNS), f32)
        for k in range(ids.shape[2]):
            hit = ids[m, :, k : k + 1] == expert
            chosen = jnp.where(hit, 1.0, chosen)
            weight = jnp.where(hit, weights[m, :, k : k + 1], weight)
        before = dot(earlier, chosen.astype(bf16), (1, 0))
        code = jnp.where((chosen > 0.0) & (before < CAPACITY), before + 1.0, 0.0)
        high, middle, low = [piece.astype(f32) for piece in exact_parts(weight)]
        values = jnp.where(kind == 0, code, jnp.where(kind == 1, high, jnp.where(kind == 2, middle, low)))
        values = jnp.where(kind < 4, values, 0.0).astype(bf16)
        for d in range(groups):
            sent[d, m, :, :part] = io[m, :, d * part : (d + 1) * part]
            sent[d, m, :, part:] = values


def home_body(moved, out):
    groups, micro, tokens, part = moved.shape
    for d in range(groups):
        for m in range(micro):
            out[m, :, d * part : (d + 1) * part] = moved[d, m]


def routing(columns, groups, experts):
    tokens = columns.shape[0]
    rows = experts * groups * CAPACITY
    row = jnp.arange(rows, dtype=jnp.int32)
    per_expert = groups * CAPACITY
    spread = (row[:, None] // per_expert == jnp.arange(experts)[None, :]).astype(bf16)
    parts = [columns[:, i * experts : (i + 1) * experts] for i in range(4)]
    code, high, middle, low = [dot(spread, part, (1, 1)) for part in parts]
    same_block = (row[:, None] % per_expert) // CAPACITY == (
        jnp.arange(tokens, dtype=jnp.int32)[None, :] // (tokens // groups)
    )
    slot = (row % CAPACITY + 1).astype(f32)
    mask = same_block & (code == slot[:, None])
    return mask.astype(bf16), jnp.where(mask, high + middle + low, 0.0)


def sum_over_dp(partial, groups):
    rows, width = partial.shape
    moved = swap(partial.reshape(groups, rows // groups, width), "dp")
    return jnp.sum(moved.astype(f32), axis=0)


def gather_over_dp(own, groups):
    moved = swap(jnp.broadcast_to(own[None], (groups,) + own.shape), "dp")
    return moved.reshape(groups * own.shape[0], own.shape[1])


def gather_and_sum(own, partial, groups):
    width = own.shape[1]
    copies = jnp.broadcast_to(own[None], (groups,) + own.shape)
    pieces = partial.reshape(groups, partial.shape[0] // groups, partial.shape[1])
    moved = swap(jnp.concatenate([copies, pieces], axis=2), "dp")
    gathered = moved[:, :, :width].reshape(groups * own.shape[0], width)
    return gathered, jnp.sum(moved[:, :, width:].astype(f32), axis=0)


def follow(values, earlier):
    return lax.optimization_barrier((values, earlier[:1, :1]))[0]


def to_experts(rows, experts):
    moved = swap(rows.reshape(experts, rows.shape[0] // experts, rows.shape[1]), "expert")
    return moved.reshape(rows.shape)


def gradients_of(grad_hidden, gate, up):
    sig = jax.nn.sigmoid(gate)
    grad_gate = (grad_hidden * up * sig * (1.0 + gate * (1.0 - sig))).astype(bf16)
    grad_up = (grad_hidden * gate * sig).astype(bf16)
    return jnp.concatenate([grad_gate, grad_up], axis=1)


def shards(layer_io, route_ids, route_weights, gate_weight, up_weight, down_weight):
    groups = lax.axis_size("dp")
    experts = lax.axis_size("expert")
    first = lax.axis_index("pipe") == 0
    micro, tokens, width = layer_io.shape[1:]
    part = width // groups
    hidden_width = gate_weight.shape[3]

    other = [trade_cores(w) for w in (gate_weight[0, 0], up_weight[0, 0], down_weight[0, 0])]
    mine = [gate_weight[0, 0], up_weight[0, 0], down_weight[0, 0]]
    layer_weights = [
        [jnp.where(first, a, b) for a, b in zip(mine, other)],
        [jnp.where(first, b, a) for a, b in zip(mine, other)],
    ]
    gate_up = [jnp.concatenate(w[:2], axis=1) for w in layer_weights]
    down = [w[2] for w in layer_weights]

    sent = local(
        functools.partial(pack_body, experts, groups),
        (groups, micro, tokens, part + ROUTE_COLUMNS),
        (layer_io[0], route_ids[0], route_weights[0]),
        "pack",
    )
    got = swap(sent.reshape(groups * micro, tokens, part + ROUTE_COLUMNS), ("dp", "pipe"))
    got = got.reshape(groups, LAYERS, tokens, part + ROUTE_COLUMNS)
    got, gate_up, down = lax.optimization_barrier((got, gate_up, down))
    inputs = got[:, 0, :, :part].reshape(groups * tokens, part)
    cotangent = got[:, 1, :, :part].reshape(groups * tokens, part)
    tables = [
        routing(got[:, l, :, part:].reshape(groups * tokens, ROUTE_COLUMNS), groups, experts)
        for l in range(LAYERS)
    ]

    scales = [jnp.sum(mixing, axis=1, keepdims=True) for _, mixing in tables]

    def two_to_experts(left, right):
        shape = (experts, left.shape[0] // experts, part)
        moved = swap(jnp.concatenate([left.reshape(shape), right.reshape(shape)], axis=1), "expert")
        return [half.reshape(left.shape) for half in jnp.split(moved, 2, axis=1)]

    def placed(l, values):
        return dot(tables[l][0], values, (1, 0))

    def mixed_in(l, values, result):
        mixed = lax.dot_general(
            tables[l][1], result.astype(f32), (((0,), (0,)), ((), ())), precision=highest
        )
        return (values.astype(f32) + mixed).astype(bf16)

    def halves(sums):
        return sums[:, :hidden_width], sums[:, hidden_width:]

    rows0, grad_out1 = two_to_experts(
        placed(0, inputs).astype(bf16), (placed(1, cotangent) * scales[1]).astype(bf16)
    )
    partial1 = dot(grad_out1, down[1], (1, 1)).astype(bf16)
    sums0 = sum_over_dp(dot(rows0, gate_up[0], (1, 0)).astype(bf16), groups)
    gate0, up0 = halves(sums0)
    own_hidden0 = follow((jax.nn.silu(gate0) * up0).astype(bf16), partial1)
    grad_hidden1 = lax.psum_scatter(partial1, "dp", scatter_dimension=0, tiled=True)
    hidden0 = gather_over_dp(own_hidden0, groups)
    hidden0, grad_hidden1 = lax.optimization_barrier((hidden0, grad_hidden1))
    result0 = to_experts(dot(hidden0, down[0], (1, 0)).astype(bf16), experts)
    middle = mixed_in(0, inputs, result0)
    rows1 = to_experts(placed(1, middle).astype(bf16), experts)
    grad_hidden1 = grad_hidden1.astype(f32)
    sums1 = sum_over_dp(dot(rows1, gate_up[1], (1, 0)).astype(bf16), groups)
    gate1, up1 = halves(sums1)
    own_hidden1 = (jax.nn.silu(gate1) * up1).astype(bf16)
    hidden1 = lax.all_gather(jnp.pad(own_hidden1, ((0, 0), (0, hidden_width))), "dp", axis=0, tiled=True)[:, :hidden_width]
    grads1 = gather_over_dp(gradients_of(grad_hidden1, gate1, up1), groups)
    back1 = to_experts(dot(grads1, gate_up[1], (1, 1)).astype(bf16), experts)
    upstream = (cotangent.astype(f32) + dot(tables[1][0], back1, (0, 0))).astype(bf16)
    grad_out0 = to_experts((placed(0, upstream) * scales[0]).astype(bf16), experts)
    grad_out0, hidden1 = lax.optimization_barrier((grad_out0, hidden1))
    partial0 = dot(grad_out0, down[0], (1, 1)).astype(bf16)
    grad_hidden0 = sum_over_dp(partial0, groups)
    grads0 = gather_over_dp(gradients_of(grad_hidden0, gate0, up0), groups)
    out1 = dot(hidden1, down[1], (1, 0)).astype(bf16)
    result1, back0 = two_to_experts(out1, dot(grads0, gate_up[0], (1, 1)).astype(bf16))
    output = mixed_in(1, middle, result1)
    upstream = (upstream.astype(f32) + dot(tables[0][0], back0, (0, 0))).astype(bf16)
    rows, grads = [rows0, rows1], [grads0, grads1]
    hidden, grad_out = [hidden0, hidden1], [grad_out0, grad_out1]

    ends = jnp.stack([upstream.reshape(groups, tokens, part), output.reshape(groups, tokens, part)], axis=1)
    home = swap(ends.reshape(groups * LAYERS, tokens, part), ("dp", "pipe"))
    home = home.reshape(groups, micro, tokens, part)
    home = local(home_body, (micro, tokens, width), (home,), "home")

    def own_and_other(pair):
        own = jnp.where(first, pair[0], pair[1])
        return own, trade_cores(jnp.where(first, pair[1], pair[0]))

    def weight_grad(left, right):
        return dot(left[0], right[0], (0, 0)) + dot(left[1], right[1], (0, 0))

    both_rows, both_grads = own_and_other(rows), own_and_other(grads)
    both_hidden, both_out = own_and_other(hidden), own_and_other(grad_out)
    grad_gate = weight_grad(both_rows, [g[:, :hidden_width] for g in both_grads])
    grad_up = weight_grad(both_rows, [g[:, hidden_width:] for g in both_grads])
    grad_down = weight_grad(both_hidden, both_out)
    return (
        home[None],
        grad_gate.astype(bf16)[None, None],
        grad_up.astype(bf16)[None, None],
        grad_down.astype(bf16)[None, None],
    )


def solution(mesh):
    tokens = P("pipe", None, ("dp", "expert"), None)
    inner = P("pipe", "expert", "dp", None)
    outer = P("pipe", "expert", None, "dp")
    return jax.shard_map(
        shards,
        mesh=mesh,
        in_specs=(tokens, tokens, tokens, inner, inner, outer),
        out_specs=(tokens, inner, inner, outer),
        check_vma=False,
    )
```

```python
import functools

import jax
import jax.numpy as jnp
from jax import lax
from jax.experimental import pallas as pl
from jax.experimental.pallas import tpu as pltpu
from jax.sharding import PartitionSpec as P

CAPACITY = 2
LAYERS = 2
ROUTE_COLUMNS = 128

highest = lax.Precision.HIGHEST
bf16 = jnp.bfloat16
f32 = jnp.float32
i32 = jnp.int32


def swap(values, axes):
    return lax.all_to_all(values, axes, split_axis=0, concat_axis=0, tiled=True)


def trade_cores(values):
    return lax.ppermute(values, "pipe", [(0, 1), (1, 0)])


def dot(a, b, contract):
    return lax.dot_general(a, b, ((contract[:1], contract[1:]), ((), ())), preferred_element_type=f32)


def local(body, dims, operands, name):
    return pl.pallas_call(
        body,
        out_shape=jax.ShapeDtypeStruct(dims, bf16),
        compiler_params=pltpu.CompilerParams(vmem_limit_bytes=32 * 1024 * 1024),
        name=name,
    )(*operands)


def exact_parts(values):
    high = values.astype(bf16)
    rest = values - high.astype(f32)
    middle = rest.astype(bf16)
    return high, middle, (rest - middle.astype(f32)).astype(bf16)


def pack_body(experts, groups, io, ids, weights, sent):
    micro, tokens, width = io.shape
    part = width // groups
    column = lax.broadcasted_iota(i32, (tokens, ROUTE_COLUMNS), 1)
    expert, kind = column % experts, column // experts
    later = lax.broadcasted_iota(i32, (tokens, tokens), 0)
    earlier = (lax.broadcasted_iota(i32, (tokens, tokens), 1) < later).astype(f32).astype(bf16)
    for m in range(micro):
        chosen = jnp.zeros((tokens, ROUTE_COLUMNS), f32)
        weight = jnp.zeros((tokens, ROUTE_COLUMNS), f32)
        for k in range(ids.shape[2]):
            hit = ids[m, :, k : k + 1] == expert
            chosen = jnp.where(hit, 1.0, chosen)
            weight = jnp.where(hit, weights[m, :, k : k + 1], weight)
        before = dot(earlier, chosen.astype(bf16), (1, 0))
        code = jnp.where((chosen > 0.0) & (before < CAPACITY), before + 1.0, 0.0)
        high, middle, low = [piece.astype(f32) for piece in exact_parts(weight)]
        values = jnp.where(kind == 0, code, jnp.where(kind == 1, high, jnp.where(kind == 2, middle, low)))
        values = jnp.where(kind < 4, values, 0.0).astype(bf16)
        for d in range(groups):
            sent[d, m, :, :part] = io[m, :, d * part : (d + 1) * part]
            sent[d, m, :, part:] = values


def home_body(moved, out):
    groups, micro, tokens, part = moved.shape
    for d in range(groups):
        for m in range(micro):
            out[m, :, d * part : (d + 1) * part] = moved[d, m]


def routing(columns, groups, experts):
    tokens = columns.shape[0]
    rows = experts * groups * CAPACITY
    row = jnp.arange(rows, dtype=jnp.int32)
    per_expert = groups * CAPACITY
    spread = (row[:, None] // per_expert == jnp.arange(experts)[None, :]).astype(bf16)
    parts = [columns[:, i * experts : (i + 1) * experts] for i in range(4)]
    code, high, middle, low = [dot(spread, part, (1, 1)) for part in parts]
    same_block = (row[:, None] % per_expert) // CAPACITY == (
        jnp.arange(tokens, dtype=jnp.int32)[None, :] // (tokens // groups)
    )
    slot = (row % CAPACITY + 1).astype(f32)
    mask = same_block & (code == slot[:, None])
    return mask.astype(bf16), jnp.where(mask, high + middle + low, 0.0)


def sum_over_dp(partial, groups):
    rows, width = partial.shape
    moved = swap(partial.reshape(groups, rows // groups, width), "dp")
    return jnp.sum(moved.astype(f32), axis=0)


def gather_over_dp(own, groups):
    moved = swap(jnp.broadcast_to(own[None], (groups,) + own.shape), "dp")
    return moved.reshape(groups * own.shape[0], own.shape[1])


def gather_and_sum(own, partial, groups):
    width = own.shape[1]
    copies = jnp.broadcast_to(own[None], (groups,) + own.shape)
    pieces = partial.reshape(groups, partial.shape[0] // groups, partial.shape[1])
    moved = swap(jnp.concatenate([copies, pieces], axis=2), "dp")
    gathered = moved[:, :, :width].reshape(groups * own.shape[0], width)
    return gathered, jnp.sum(moved[:, :, width:].astype(f32), axis=0)


def follow(values, earlier):
    return lax.optimization_barrier((values, earlier[:1, :1]))[0]


def to_experts(rows, experts):
    moved = swap(rows.reshape(experts, rows.shape[0] // experts, rows.shape[1]), "expert")
    return moved.reshape(rows.shape)


def gradients_of(grad_hidden, gate, up):
    sig = jax.nn.sigmoid(gate)
    grad_gate = (grad_hidden * up * sig * (1.0 + gate * (1.0 - sig))).astype(bf16)
    grad_up = (grad_hidden * gate * sig).astype(bf16)
    return jnp.concatenate([grad_gate, grad_up], axis=1)


def shards(layer_io, route_ids, route_weights, gate_weight, up_weight, down_weight):
    groups = lax.axis_size("dp")
    experts = lax.axis_size("expert")
    first = lax.axis_index("pipe") == 0
    micro, tokens, width = layer_io.shape[1:]
    part = width // groups
    hidden_width = gate_weight.shape[3]

    other = [trade_cores(w) for w in (gate_weight[0, 0], up_weight[0, 0], down_weight[0, 0])]
    mine = [gate_weight[0, 0], up_weight[0, 0], down_weight[0, 0]]
    layer_weights = [
        [jnp.where(first, a, b) for a, b in zip(mine, other)],
        [jnp.where(first, b, a) for a, b in zip(mine, other)],
    ]
    gate_up = [jnp.concatenate(w[:2], axis=1) for w in layer_weights]
    down = [w[2] for w in layer_weights]

    sent = local(
        functools.partial(pack_body, experts, groups),
        (groups, micro, tokens, part + ROUTE_COLUMNS),
        (layer_io[0], route_ids[0], route_weights[0]),
        "pack",
    )
    got = swap(sent.reshape(groups * micro, tokens, part + ROUTE_COLUMNS), ("dp", "pipe"))
    got = got.reshape(groups, LAYERS, tokens, part + ROUTE_COLUMNS)
    got, gate_up, down = lax.optimization_barrier((got, gate_up, down))
    inputs = got[:, 0, :, :part].reshape(groups * tokens, part)
    cotangent = got[:, 1, :, :part].reshape(groups * tokens, part)
    tables = [
        routing(got[:, l, :, part:].reshape(groups * tokens, ROUTE_COLUMNS), groups, experts)
        for l in range(LAYERS)
    ]

    scales = [jnp.sum(mixing, axis=1, keepdims=True) for _, mixing in tables]

    def two_to_experts(left, right):
        shape = (experts, left.shape[0] // experts, part)
        moved = swap(jnp.concatenate([left.reshape(shape), right.reshape(shape)], axis=1), "expert")
        return [half.reshape(left.shape) for half in jnp.split(moved, 2, axis=1)]

    def placed(l, values):
        return dot(tables[l][0], values, (1, 0))

    def mixed_in(l, values, result):
        mixed = lax.dot_general(
            tables[l][1], result.astype(f32), (((0,), (0,)), ((), ())), precision=highest
        )
        return (values.astype(f32) + mixed).astype(bf16)

    def halves(sums):
        return sums[:, :hidden_width], sums[:, hidden_width:]

    rows0, grad_out1 = two_to_experts(
        placed(0, inputs).astype(bf16), (placed(1, cotangent) * scales[1]).astype(bf16)
    )
    partial1 = dot(grad_out1, down[1], (1, 1)).astype(bf16)
    sums0 = sum_over_dp(dot(rows0, gate_up[0], (1, 0)).astype(bf16), groups)
    gate0, up0 = halves(sums0)
    own_hidden0 = follow((jax.nn.silu(gate0) * up0).astype(bf16), partial1)
    grad_hidden1 = lax.psum_scatter(partial1, "dp", scatter_dimension=0, tiled=True)
    hidden0 = gather_over_dp(own_hidden0, groups)
    hidden0, grad_hidden1 = lax.optimization_barrier((hidden0, grad_hidden1))
    result0 = to_experts(dot(hidden0, down[0], (1, 0)).astype(bf16), experts)
    middle = mixed_in(0, inputs, result0)
    rows1 = to_experts(placed(1, middle).astype(bf16), experts)
    grad_hidden1 = grad_hidden1.astype(f32)
    sums1 = sum_over_dp(dot(rows1, gate_up[1], (1, 0)).astype(bf16), groups)
    gate1, up1 = halves(sums1)
    own_hidden1 = (jax.nn.silu(gate1) * up1).astype(bf16)
    beside = jnp.concatenate([own_hidden1, sums0.astype(bf16)], axis=1)
    beside = lax.all_gather(beside, "dp", axis=0, tiled=True)
    grads1 = gather_over_dp(gradients_of(grad_hidden1, gate1, up1), groups)
    back1 = to_experts(dot(grads1, gate_up[1], (1, 1)).astype(bf16), experts)
    upstream = (cotangent.astype(f32) + dot(tables[1][0], back1, (0, 0))).astype(bf16)
    grad_out0 = to_experts((placed(0, upstream) * scales[0]).astype(bf16), experts)
    grad_out0, beside = lax.optimization_barrier((grad_out0, beside))
    hidden1, all_gate0, all_up0 = [
        beside[:, i * hidden_width : (i + 1) * hidden_width] for i in range(3)
    ]
    partial0 = dot(grad_out0, down[0], (1, 1)).astype(bf16)
    grad_hidden0 = sum_over_dp(partial0, groups)
    all_grad_hidden0 = gather_over_dp(grad_hidden0.astype(bf16), groups)
    grads0 = gradients_of(all_grad_hidden0.astype(f32), all_gate0.astype(f32), all_up0.astype(f32))
    out1 = dot(hidden1, down[1], (1, 0)).astype(bf16)
    result1, back0 = two_to_experts(out1, dot(grads0, gate_up[0], (1, 1)).astype(bf16))
    output = mixed_in(1, middle, result1)
    upstream = (upstream.astype(f32) + dot(tables[0][0], back0, (0, 0))).astype(bf16)
    rows, grads = [rows0, rows1], [grads0, grads1]
    hidden, grad_out = [hidden0, hidden1], [grad_out0, grad_out1]

    ends = jnp.stack([upstream.reshape(groups, tokens, part), output.reshape(groups, tokens, part)], axis=1)
    home = swap(ends.reshape(groups * LAYERS, tokens, part), ("dp", "pipe"))
    home = home.reshape(groups, micro, tokens, part)
    home = local(home_body, (micro, tokens, width), (home,), "home")

    def own_and_other(pair):
        own = jnp.where(first, pair[0], pair[1])
        return own, trade_cores(jnp.where(first, pair[1], pair[0]))

    def weight_grad(left, right):
        return dot(left[0], right[0], (0, 0)) + dot(left[1], right[1], (0, 0))

    both_rows, both_grads = own_and_other(rows), own_and_other(grads)
    both_hidden, both_out = own_and_other(hidden), own_and_other(grad_out)
    grad_gate = weight_grad(both_rows, [g[:, :hidden_width] for g in both_grads])
    grad_up = weight_grad(both_rows, [g[:, hidden_width:] for g in both_grads])
    grad_down = weight_grad(both_hidden, both_out)
    return (
        home[None],
        grad_gate.astype(bf16)[None, None],
        grad_up.astype(bf16)[None, None],
        grad_down.astype(bf16)[None, None],
    )


def solution(mesh):
    tokens = P("pipe", None, ("dp", "expert"), None)
    inner = P("pipe", "expert", "dp", None)
    outer = P("pipe", "expert", None, "dp")
    return jax.shard_map(
        shards,
        mesh=mesh,
        in_specs=(tokens, tokens, tokens, inner, inner, outer),
        out_specs=(tokens, inner, inner, outer),
        check_vma=False,
    )
```

```python
import functools

import jax
import jax.numpy as jnp
from jax import lax
from jax.experimental import pallas as pl
from jax.experimental.pallas import tpu as pltpu
from jax.sharding import PartitionSpec as P

CAPACITY = 2
LAYERS = 2
ROUTE_COLUMNS = 128

highest = lax.Precision.HIGHEST
bf16 = jnp.bfloat16
f32 = jnp.float32
i32 = jnp.int32


def swap(values, axes):
    return lax.all_to_all(values, axes, split_axis=0, concat_axis=0, tiled=True)


def trade_cores(values):
    return lax.ppermute(values, "pipe", [(0, 1), (1, 0)])


def dot(a, b, contract):
    return lax.dot_general(a, b, ((contract[:1], contract[1:]), ((), ())), preferred_element_type=f32)


def local(body, dims, operands, name):
    return pl.pallas_call(
        body,
        out_shape=jax.ShapeDtypeStruct(dims, bf16),
        compiler_params=pltpu.CompilerParams(vmem_limit_bytes=32 * 1024 * 1024),
        name=name,
    )(*operands)


def exact_parts(values):
    high = values.astype(bf16)
    rest = values - high.astype(f32)
    middle = rest.astype(bf16)
    return high, middle, (rest - middle.astype(f32)).astype(bf16)


def pack_body(experts, groups, io, ids, weights, sent):
    micro, top, tokens = ids.shape
    part = io.shape[2] // groups
    dims = (ROUTE_COLUMNS, tokens)
    column = lax.broadcasted_iota(i32, dims, 0)
    expert, kind = column % experts, column // experts
    square = (tokens, tokens)
    row, lane = lax.broadcasted_iota(i32, square, 0), lax.broadcasted_iota(i32, square, 1)
    earlier = (row < lane).astype(f32).astype(bf16)
    same = (row == lane).astype(f32).astype(bf16)
    for m in range(micro):
        chosen = jnp.zeros(dims, f32)
        weight = jnp.zeros(dims, f32)
        for k in range(top):
            hit = ids[m, k : k + 1, :] == expert
            chosen = jnp.where(hit, 1.0, chosen)
            weight = jnp.where(hit, weights[m, k : k + 1, :], weight)
        before = dot(chosen.astype(bf16), earlier, (1, 0))
        code = jnp.where((chosen > 0.0) & (before < CAPACITY), before + 1.0, 0.0)
        high, middle, low = [piece.astype(f32) for piece in exact_parts(weight)]
        values = jnp.where(kind == 0, code, jnp.where(kind == 1, high, jnp.where(kind == 2, middle, low)))
        values = jnp.where(kind < 4, values, 0.0).astype(bf16)
        values = dot(same, values, (1, 1)).astype(bf16)
        for d in range(groups):
            sent[d, m, :, :part] = io[m, :, d * part : (d + 1) * part]
            sent[d, m, :, part:] = values


def home_body(moved, out):
    groups, micro, tokens, part = moved.shape
    for d in range(groups):
        for m in range(micro):
            out[m, :, d * part : (d + 1) * part] = moved[d, m]


def routing(columns, groups, experts):
    tokens = columns.shape[0]
    rows = experts * groups * CAPACITY
    row = jnp.arange(rows, dtype=jnp.int32)
    per_expert = groups * CAPACITY
    spread = (row[:, None] // per_expert == jnp.arange(experts)[None, :]).astype(bf16)
    parts = [columns[:, i * experts : (i + 1) * experts] for i in range(4)]
    code, high, middle, low = [dot(spread, part, (1, 1)) for part in parts]
    same_block = (row[:, None] % per_expert) // CAPACITY == (
        jnp.arange(tokens, dtype=jnp.int32)[None, :] // (tokens // groups)
    )
    slot = (row % CAPACITY + 1).astype(f32)
    mask = same_block & (code == slot[:, None])
    return mask.astype(bf16), jnp.where(mask, high + middle + low, 0.0)


def sum_over_dp(partial, groups):
    rows, width = partial.shape
    moved = swap(partial.reshape(groups, rows // groups, width), "dp")
    return jnp.sum(moved.astype(f32), axis=0)


def gather_over_dp(own, groups):
    moved = swap(jnp.broadcast_to(own[None], (groups,) + own.shape), "dp")
    return moved.reshape(groups * own.shape[0], own.shape[1])


def gather_and_sum(own, partial, groups):
    width = own.shape[1]
    copies = jnp.broadcast_to(own[None], (groups,) + own.shape)
    pieces = partial.reshape(groups, partial.shape[0] // groups, partial.shape[1])
    moved = swap(jnp.concatenate([copies, pieces], axis=2), "dp")
    gathered = moved[:, :, :width].reshape(groups * own.shape[0], width)
    return gathered, jnp.sum(moved[:, :, width:].astype(f32), axis=0)


def follow(values, earlier):
    return lax.optimization_barrier((values, earlier[:1, :1]))[0]


def to_experts(rows, experts):
    moved = swap(rows.reshape(experts, rows.shape[0] // experts, rows.shape[1]), "expert")
    return moved.reshape(rows.shape)


def gradients_of(grad_hidden, gate, up):
    sig = jax.nn.sigmoid(gate)
    grad_gate = (grad_hidden * up * sig * (1.0 + gate * (1.0 - sig))).astype(bf16)
    grad_up = (grad_hidden * gate * sig).astype(bf16)
    return jnp.concatenate([grad_gate, grad_up], axis=1)


def shards(layer_io, route_ids, route_weights, gate_weight, up_weight, down_weight):
    groups = lax.axis_size("dp")
    experts = lax.axis_size("expert")
    first = lax.axis_index("pipe") == 0
    micro, tokens, width = layer_io.shape[1:]
    part = width // groups
    hidden_width = gate_weight.shape[3]

    other = [trade_cores(w) for w in (gate_weight[0, 0], up_weight[0, 0], down_weight[0, 0])]
    mine = [gate_weight[0, 0], up_weight[0, 0], down_weight[0, 0]]
    layer_weights = [
        [jnp.where(first, a, b) for a, b in zip(mine, other)],
        [jnp.where(first, b, a) for a, b in zip(mine, other)],
    ]
    gate_up = [jnp.concatenate(w[:2], axis=1) for w in layer_weights]
    down = [w[2] for w in layer_weights]

    sent = local(
        functools.partial(pack_body, experts, groups),
        (groups, micro, tokens, part + ROUTE_COLUMNS),
        (layer_io[0], route_ids[0].swapaxes(1, 2), route_weights[0].swapaxes(1, 2)),
        "pack",
    )
    got = swap(sent.reshape(groups * micro, tokens, part + ROUTE_COLUMNS), ("dp", "pipe"))
    got = got.reshape(groups, LAYERS, tokens, part + ROUTE_COLUMNS)
    got, gate_up, down = lax.optimization_barrier((got, gate_up, down))
    inputs = got[:, 0, :, :part].reshape(groups * tokens, part)
    cotangent = got[:, 1, :, :part].reshape(groups * tokens, part)
    tables = [
        routing(got[:, l, :, part:].reshape(groups * tokens, ROUTE_COLUMNS), groups, experts)
        for l in range(LAYERS)
    ]

    scales = [jnp.sum(mixing, axis=1, keepdims=True) for _, mixing in tables]

    def two_to_experts(left, right):
        shape = (experts, left.shape[0] // experts, part)
        moved = swap(jnp.concatenate([left.reshape(shape), right.reshape(shape)], axis=1), "expert")
        return [half.reshape(left.shape) for half in jnp.split(moved, 2, axis=1)]

    def placed(l, values):
        return dot(tables[l][0], values, (1, 0))

    def mixed_in(l, values, result):
        mixed = lax.dot_general(
            tables[l][1], result.astype(f32), (((0,), (0,)), ((), ())), precision=highest
        )
        return (values.astype(f32) + mixed).astype(bf16)

    def halves(sums):
        return sums[:, :hidden_width], sums[:, hidden_width:]

    rows0, grad_out1 = two_to_experts(
        placed(0, inputs).astype(bf16), (placed(1, cotangent) * scales[1]).astype(bf16)
    )
    partial1 = dot(grad_out1, down[1], (1, 1)).astype(bf16)
    sums0 = sum_over_dp(dot(rows0, gate_up[0], (1, 0)).astype(bf16), groups)
    gate0, up0 = halves(sums0)
    own_hidden0 = follow((jax.nn.silu(gate0) * up0).astype(bf16), partial1)
    grad_hidden1 = lax.psum_scatter(partial1, "dp", scatter_dimension=0, tiled=True)
    hidden0 = gather_over_dp(own_hidden0, groups)
    hidden0, grad_hidden1 = lax.optimization_barrier((hidden0, grad_hidden1))
    result0 = to_experts(dot(hidden0, down[0], (1, 0)).astype(bf16), experts)
    middle = mixed_in(0, inputs, result0)
    rows1 = to_experts(placed(1, middle).astype(bf16), experts)
    grad_hidden1 = grad_hidden1.astype(f32)
    sums1 = sum_over_dp(dot(rows1, gate_up[1], (1, 0)).astype(bf16), groups)
    gate1, up1 = halves(sums1)
    own_hidden1 = (jax.nn.silu(gate1) * up1).astype(bf16)
    beside = jnp.concatenate([own_hidden1, sums0.astype(bf16)], axis=1)
    beside = lax.all_gather(beside, "dp", axis=0, tiled=True)
    grads1 = gather_over_dp(gradients_of(grad_hidden1, gate1, up1), groups)
    back1 = to_experts(dot(grads1, gate_up[1], (1, 1)).astype(bf16), experts)
    upstream = (cotangent.astype(f32) + dot(tables[1][0], back1, (0, 0))).astype(bf16)
    grad_out0 = to_experts((placed(0, upstream) * scales[0]).astype(bf16), experts)
    grad_out0, beside = lax.optimization_barrier((grad_out0, beside))
    hidden1, all_gate0, all_up0 = [
        beside[:, i * hidden_width : (i + 1) * hidden_width] for i in range(3)
    ]
    partial0 = dot(grad_out0, down[0], (1, 1)).astype(bf16)
    grad_hidden0 = sum_over_dp(partial0, groups)
    all_grad_hidden0 = gather_over_dp(grad_hidden0.astype(bf16), groups)
    grads0 = gradients_of(all_grad_hidden0.astype(f32), all_gate0.astype(f32), all_up0.astype(f32))
    out1 = dot(hidden1, down[1], (1, 0)).astype(bf16)
    result1, back0 = two_to_experts(out1, dot(grads0, gate_up[0], (1, 1)).astype(bf16))
    output = mixed_in(1, middle, result1)
    upstream = (upstream.astype(f32) + dot(tables[0][0], back0, (0, 0))).astype(bf16)
    rows, grads = [rows0, rows1], [grads0, grads1]
    hidden, grad_out = [hidden0, hidden1], [grad_out0, grad_out1]

    ends = jnp.stack([upstream.reshape(groups, tokens, part), output.reshape(groups, tokens, part)], axis=1)
    home = swap(ends.reshape(groups * LAYERS, tokens, part), ("dp", "pipe"))
    home = home.reshape(groups, micro, tokens, part)
    home = local(home_body, (micro, tokens, width), (home,), "home")

    def own_and_other(pair):
        own = jnp.where(first, pair[0], pair[1])
        return own, trade_cores(jnp.where(first, pair[1], pair[0]))

    def weight_grad(left, right):
        return dot(left[0], right[0], (0, 0)) + dot(left[1], right[1], (0, 0))

    both_rows, both_grads = own_and_other(rows), own_and_other(grads)
    both_hidden, both_out = own_and_other(hidden), own_and_other(grad_out)
    grad_gate = weight_grad(both_rows, [g[:, :hidden_width] for g in both_grads])
    grad_up = weight_grad(both_rows, [g[:, hidden_width:] for g in both_grads])
    grad_down = weight_grad(both_hidden, both_out)
    return (
        home[None],
        grad_gate.astype(bf16)[None, None],
        grad_up.astype(bf16)[None, None],
        grad_down.astype(bf16)[None, None],
    )


def solution(mesh):
    tokens = P("pipe", None, ("dp", "expert"), None)
    inner = P("pipe", "expert", "dp", None)
    outer = P("pipe", "expert", None, "dp")
    return jax.shard_map(
        shards,
        mesh=mesh,
        in_specs=(tokens, tokens, tokens, inner, inner, outer),
        out_specs=(tokens, inner, inner, outer),
        check_vma=False,
    )
```

```python
import functools

import jax
import jax.numpy as jnp
from jax import lax
from jax.experimental import pallas as pl
from jax.experimental.pallas import tpu as pltpu
from jax.sharding import PartitionSpec as P

CAPACITY = 2
LAYERS = 2
ROUTE_COLUMNS = 128

combining = lax.Precision.HIGH
bf16 = jnp.bfloat16
f32 = jnp.float32
i32 = jnp.int32


def swap(values, axes):
    return lax.all_to_all(values, axes, split_axis=0, concat_axis=0, tiled=True)


def trade_cores(values):
    return lax.ppermute(values, "pipe", [(0, 1), (1, 0)])


def dot(a, b, contract):
    return lax.dot_general(a, b, ((contract[:1], contract[1:]), ((), ())), preferred_element_type=f32)


def local(body, dims, operands, name):
    return pl.pallas_call(
        body,
        out_shape=jax.ShapeDtypeStruct(dims, bf16),
        compiler_params=pltpu.CompilerParams(vmem_limit_bytes=32 * 1024 * 1024),
        name=name,
    )(*operands)


def exact_parts(values):
    high = values.astype(bf16)
    rest = values - high.astype(f32)
    middle = rest.astype(bf16)
    return high, middle, (rest - middle.astype(f32)).astype(bf16)


def pack_body(experts, groups, io, ids, weights, sent):
    micro, top, tokens = ids.shape
    part = io.shape[2] // groups
    dims = (ROUTE_COLUMNS, tokens)
    column = lax.broadcasted_iota(i32, dims, 0)
    expert, kind = column % experts, column // experts
    square = (tokens, tokens)
    row, lane = lax.broadcasted_iota(i32, square, 0), lax.broadcasted_iota(i32, square, 1)
    earlier = (row < lane).astype(f32).astype(bf16)
    same = (row == lane).astype(f32).astype(bf16)
    for m in range(micro):
        chosen = jnp.zeros(dims, f32)
        weight = jnp.zeros(dims, f32)
        for k in range(top):
            hit = ids[m, k : k + 1, :] == expert
            chosen = jnp.where(hit, 1.0, chosen)
            weight = jnp.where(hit, weights[m, k : k + 1, :], weight)
        before = dot(chosen.astype(bf16), earlier, (1, 0))
        code = jnp.where((chosen > 0.0) & (before < CAPACITY), before + 1.0, 0.0)
        high, middle, low = [piece.astype(f32) for piece in exact_parts(weight)]
        values = jnp.where(kind == 0, code, jnp.where(kind == 1, high, jnp.where(kind == 2, middle, low)))
        values = jnp.where(kind < 4, values, 0.0).astype(bf16)
        values = dot(same, values, (1, 1)).astype(bf16)
        for d in range(groups):
            sent[d, m, :, :part] = io[m, :, d * part : (d + 1) * part]
            sent[d, m, :, part:] = values


def home_body(moved, out):
    groups, micro, tokens, part = moved.shape
    for d in range(groups):
        for m in range(micro):
            out[m, :, d * part : (d + 1) * part] = moved[d, m]


def routing(columns, groups, experts):
    tokens = columns.shape[0]
    rows = experts * groups * CAPACITY
    row = jnp.arange(rows, dtype=jnp.int32)
    per_expert = groups * CAPACITY
    spread = (row[:, None] // per_expert == jnp.arange(experts)[None, :]).astype(bf16)
    parts = [columns[:, i * experts : (i + 1) * experts] for i in range(4)]
    code, high, middle, low = [dot(spread, part, (1, 1)) for part in parts]
    same_block = (row[:, None] % per_expert) // CAPACITY == (
        jnp.arange(tokens, dtype=jnp.int32)[None, :] // (tokens // groups)
    )
    slot = (row % CAPACITY + 1).astype(f32)
    mask = same_block & (code == slot[:, None])
    return mask.astype(bf16), jnp.where(mask, high + middle + low, 0.0)


def sum_over_dp(partial, groups):
    rows, width = partial.shape
    moved = swap(partial.reshape(groups, rows // groups, width), "dp")
    return jnp.sum(moved.astype(f32), axis=0)


def gather_over_dp(own, groups):
    moved = swap(jnp.broadcast_to(own[None], (groups,) + own.shape), "dp")
    return moved.reshape(groups * own.shape[0], own.shape[1])


def gather_and_sum(own, partial, groups):
    width = own.shape[1]
    copies = jnp.broadcast_to(own[None], (groups,) + own.shape)
    pieces = partial.reshape(groups, partial.shape[0] // groups, partial.shape[1])
    moved = swap(jnp.concatenate([copies, pieces], axis=2), "dp")
    gathered = moved[:, :, :width].reshape(groups * own.shape[0], width)
    return gathered, jnp.sum(moved[:, :, width:].astype(f32), axis=0)


def follow(values, earlier):
    return lax.optimization_barrier((values, earlier[:1, :1]))[0]


def to_experts(rows, experts):
    moved = swap(rows.reshape(experts, rows.shape[0] // experts, rows.shape[1]), "expert")
    return moved.reshape(rows.shape)


def gradients_of(grad_hidden, gate, up):
    sig = jax.nn.sigmoid(gate)
    grad_gate = (grad_hidden * up * sig * (1.0 + gate * (1.0 - sig))).astype(bf16)
    grad_up = (grad_hidden * gate * sig).astype(bf16)
    return jnp.concatenate([grad_gate, grad_up], axis=1)


def shards(layer_io, route_ids, route_weights, gate_weight, up_weight, down_weight):
    groups = lax.axis_size("dp")
    experts = lax.axis_size("expert")
    first = lax.axis_index("pipe") == 0
    micro, tokens, width = layer_io.shape[1:]
    part = width // groups
    hidden_width = gate_weight.shape[3]

    other = [trade_cores(w) for w in (gate_weight[0, 0], up_weight[0, 0], down_weight[0, 0])]
    mine = [gate_weight[0, 0], up_weight[0, 0], down_weight[0, 0]]
    layer_weights = [
        [jnp.where(first, a, b) for a, b in zip(mine, other)],
        [jnp.where(first, b, a) for a, b in zip(mine, other)],
    ]
    gate_up = [jnp.concatenate(w[:2], axis=1) for w in layer_weights]
    down = [w[2] for w in layer_weights]

    sent = local(
        functools.partial(pack_body, experts, groups),
        (groups, micro, tokens, part + ROUTE_COLUMNS),
        (layer_io[0], route_ids[0].swapaxes(1, 2), route_weights[0].swapaxes(1, 2)),
        "pack",
    )
    got = swap(sent.reshape(groups * micro, tokens, part + ROUTE_COLUMNS), ("dp", "pipe"))
    got = got.reshape(groups, LAYERS, tokens, part + ROUTE_COLUMNS)
    got, gate_up, down = lax.optimization_barrier((got, gate_up, down))
    inputs = got[:, 0, :, :part].reshape(groups * tokens, part)
    cotangent = got[:, 1, :, :part].reshape(groups * tokens, part)
    tables = [
        routing(got[:, l, :, part:].reshape(groups * tokens, ROUTE_COLUMNS), groups, experts)
        for l in range(LAYERS)
    ]

    scales = [jnp.sum(mixing, axis=1, keepdims=True) for _, mixing in tables]

    def two_to_experts(left, right):
        shape = (experts, left.shape[0] // experts, part)
        moved = swap(jnp.concatenate([left.reshape(shape), right.reshape(shape)], axis=1), "expert")
        return [half.reshape(left.shape) for half in jnp.split(moved, 2, axis=1)]

    def placed(l, values):
        return dot(tables[l][0], values, (1, 0))

    def mixed_in(l, values, result):
        mixed = lax.dot_general(
            tables[l][1], result.astype(f32), (((0,), (0,)), ((), ())), precision=combining
        )
        return (values.astype(f32) + mixed).astype(bf16)

    def halves(sums):
        return sums[:, :hidden_width], sums[:, hidden_width:]

    rows0, grad_out1 = two_to_experts(
        placed(0, inputs).astype(bf16), (placed(1, cotangent) * scales[1]).astype(bf16)
    )
    partial1 = dot(grad_out1, down[1], (1, 1)).astype(bf16)
    sums0 = sum_over_dp(dot(rows0, gate_up[0], (1, 0)).astype(bf16), groups)
    gate0, up0 = halves(sums0)
    own_hidden0 = follow((jax.nn.silu(gate0) * up0).astype(bf16), partial1)
    grad_hidden1 = lax.psum_scatter(partial1, "dp", scatter_dimension=0, tiled=True)
    hidden0 = gather_over_dp(own_hidden0, groups)
    hidden0, grad_hidden1 = lax.optimization_barrier((hidden0, grad_hidden1))
    result0 = to_experts(dot(hidden0, down[0], (1, 0)).astype(bf16), experts)
    middle = mixed_in(0, inputs, result0)
    rows1 = to_experts(placed(1, middle).astype(bf16), experts)
    grad_hidden1 = grad_hidden1.astype(f32)
    sums1 = sum_over_dp(dot(rows1, gate_up[1], (1, 0)).astype(bf16), groups)
    gate1, up1 = halves(sums1)
    own_hidden1 = (jax.nn.silu(gate1) * up1).astype(bf16)
    beside = jnp.concatenate([own_hidden1, sums0.astype(bf16)], axis=1)
    beside = lax.all_gather(beside, "dp", axis=0, tiled=True)
    grads1 = gather_over_dp(gradients_of(grad_hidden1, gate1, up1), groups)
    back1 = to_experts(dot(grads1, gate_up[1], (1, 1)).astype(bf16), experts)
    upstream = (cotangent.astype(f32) + dot(tables[1][0], back1, (0, 0))).astype(bf16)
    grad_out0 = to_experts((placed(0, upstream) * scales[0]).astype(bf16), experts)
    grad_out0, beside = lax.optimization_barrier((grad_out0, beside))
    hidden1, all_gate0, all_up0 = [
        beside[:, i * hidden_width : (i + 1) * hidden_width] for i in range(3)
    ]
    partial0 = dot(grad_out0, down[0], (1, 1)).astype(bf16)
    grad_hidden0 = sum_over_dp(partial0, groups)
    all_grad_hidden0 = gather_over_dp(grad_hidden0.astype(bf16), groups)
    grads0 = gradients_of(all_grad_hidden0.astype(f32), all_gate0.astype(f32), all_up0.astype(f32))
    out1 = dot(hidden1, down[1], (1, 0)).astype(bf16)
    result1, back0 = two_to_experts(out1, dot(grads0, gate_up[0], (1, 1)).astype(bf16))
    output = mixed_in(1, middle, result1)
    upstream = (upstream.astype(f32) + dot(tables[0][0], back0, (0, 0))).astype(bf16)
    rows, grads = [rows0, rows1], [grads0, grads1]
    hidden, grad_out = [hidden0, hidden1], [grad_out0, grad_out1]

    ends = jnp.stack([upstream.reshape(groups, tokens, part), output.reshape(groups, tokens, part)], axis=1)
    home = swap(ends.reshape(groups * LAYERS, tokens, part), ("dp", "pipe"))
    home = home.reshape(groups, micro, tokens, part)
    home = local(home_body, (micro, tokens, width), (home,), "home")

    def own_and_other(pair):
        own = jnp.where(first, pair[0], pair[1])
        return own, trade_cores(jnp.where(first, pair[1], pair[0]))

    def weight_grad(left, right):
        return dot(left[0], right[0], (0, 0)) + dot(left[1], right[1], (0, 0))

    both_rows, both_grads = own_and_other(rows), own_and_other(grads)
    both_hidden, both_out = own_and_other(hidden), own_and_other(grad_out)
    grad_gate = weight_grad(both_rows, [g[:, :hidden_width] for g in both_grads])
    grad_up = weight_grad(both_rows, [g[:, hidden_width:] for g in both_grads])
    grad_down = weight_grad(both_hidden, both_out)
    return (
        home[None],
        grad_gate.astype(bf16)[None, None],
        grad_up.astype(bf16)[None, None],
        grad_down.astype(bf16)[None, None],
    )


def solution(mesh):
    tokens = P("pipe", None, ("dp", "expert"), None)
    inner = P("pipe", "expert", "dp", None)
    outer = P("pipe", "expert", None, "dp")
    return jax.shard_map(
        shards,
        mesh=mesh,
        in_specs=(tokens, tokens, tokens, inner, inner, outer),
        out_specs=(tokens, inner, inner, outer),
        check_vma=False,
    )
```
